32 devices in a mesh: groups: 2 (over x), wide: 16 (over z, y, core).
Axes of the slice: x: 2, y: 2, z: 4, core: 2. Of those that a mesh axis runs over, the one named last changes fastest.
Arguments:
- queries: bfloat16 [128, 32, 128], P(('groups', 'wide')), parts along dimension 0, may hold values from -6 to 6
- candidates: int32 [128, 192], P('groups', 'wide'), parts along dimension 0, may hold values from -1 to 47, as said below
- codes: int32 [1536, 128], P(('groups', 'wide')), parts along dimension 0, may hold values from 0 to 4095
- residual_words: int32 [1536, 16, 128], P(('groups', 'wide')), parts along dimension 0, may hold values from 0 to 65535
- lengths: int32 [1536], P(('groups', 'wide')), parts along dimension 0, may hold values from 32 to 128, as said below
- centroids: float32 [131072, 128], P(('groups', 'wide')), parts along dimension 0, may hold values from -0.5 to 0.5
- bucket_values: float32 [4, 128], replicated, may hold values from -0.35355338 to 0.35355338
Outputs:
- scores: float32 [128, 192], P(('groups', 'wide')), parts along dimension 0
The draws below stay inside these ranges and needn't reach their ends.
There are 2 independent parts, one for each index of `groups`. The reference program is written for one: setup_inputs(seed, part) draws one part's arguments, and reference() takes and returns one part's arrays. A program takes and returns all parts, laid end to end along the dimension named above; an argument that names none is the same for every part. Nothing has to cross between parts.
Inputs may be any that keep to these rules, and one draw needn't show every extreme that they name: `candidates`: -1 marks an empty slot; in each block of 12 slots of one query at one shard the live slots come first, and every query fills all 12 slots at some shard. `lengths`: every shard holds a passage of 128 tokens.
All inputs are finite; a program needn't handle non-finite values.
Results may differ from the reference program's by a relative error of at most 0.00034.
Values may be sent and summed in bfloat16 or wider, within the bound.
A program may use at most 64 MiB of HBM per device.

```python
import jax
import jax.numpy as jnp
from jax import lax

D = 128
QT = 32
PLEN = 128
CENT_DEV = 4096
CAND = 12
P_DEV = 48
RWORDS = 16
QUERIES = 64
PASSAGES = 768
CENTROIDS = 65536
SLOTS = 192
N_WIDE = 16


def draw_candidates(key, part):
    key = jax.random.fold_in(key, 11)
    key_hot, key_count, key_full, key_ids = jax.random.split(key, 4)
    owners = SLOTS // CAND
    hotness = jax.random.randint(key_hot, (owners,), 1, 5)
    counts = jax.random.randint(key_count, (QUERIES, owners), 0, 1 << 20) % (hotness[None, :] * CAND // 2 + 1)
    counts = jnp.minimum(counts, CAND)
    full_owner = jax.random.randint(key_full, (QUERIES,), 0, owners)
    counts = jnp.where(jnp.arange(owners)[None, :] == full_owner[:, None], CAND, counts)
    passage_ids = jax.random.randint(key_ids, (QUERIES, owners, CAND), 0, P_DEV)
    slot_index = jnp.arange(CAND)[None, None, :]
    chosen = jnp.where(slot_index < counts[:, :, None], passage_ids, -1)
    return chosen.reshape(QUERIES, SLOTS).astype(jnp.int32)


def draw_residual_words(key, part):
    key = jax.random.fold_in(key, 23)
    packed = jax.random.randint(key, (PASSAGES, RWORDS, PLEN), 0, 2 ** 16)
    packed = packed.at[0, 0, 0].set(2 ** 16 - 1)
    return packed.astype(jnp.int32)


def draw_lengths(key, part):
    key = jax.random.fold_in(key, 37)
    key_len, key_full = jax.random.split(key)
    drawn = jax.random.randint(key_len, (PASSAGES,), PLEN // 4, PLEN + 1)
    full_slot = jax.random.randint(key_full, (PASSAGES // P_DEV,), 0, P_DEV)
    index = jnp.arange(PASSAGES)
    chosen = jnp.where(index % P_DEV == full_slot[index // P_DEV], PLEN, drawn)
    return chosen.astype(jnp.int32)


def plant(values, key, least, top_value):
    shape = values.shape
    spot = [jax.random.randint(jax.random.fold_in(key, axis), (), 0, shape[axis]) for axis in range(len(shape))]
    values = values.at[tuple(spot)].set(least)
    longest = shape.index(max(shape))
    spot[longest] = (spot[longest] + 1) % shape[longest]
    return values.at[tuple(spot)].set(top_value)


def level_of(key, extent, shards, smallest, top_value):
    def one(position, blocks):
        draws = jax.random.uniform(jax.random.fold_in(jax.random.fold_in(key, 6), position), (blocks,), jnp.float32, smallest / len(shards), top_value / len(shards))
        return jnp.repeat(jnp.exp(draws), extent[position] // blocks).reshape((-1,) + (1,) * (len(extent) - position - 1))

    loudness = one(*shards[0])
    for cut in shards[1:]:
        loudness = loudness * one(*cut)
    return loudness


def centred(stream_key, shape, deviation, most, pieces=(), held_as=jnp.bfloat16):
    array = jax.random.normal(stream_key, shape, jnp.float32) * deviation
    if len(pieces) > 0:
        array = level_of(stream_key, shape, pieces, -0.22, 0.18) * array
    return jnp.clip(array, min=-most, max=most).astype(held_as)


def setup_inputs(seed: int = 0, part: int = 0) -> dict:
    key_list = jax.random.split(jax.random.key(seed), 8)
    part_keys = jax.random.split(jax.random.fold_in(key_list[7], part), 8)
    queries = centred(part_keys[0], (QUERIES, QT, D), 1.0, 6.0, ((0, 16),))
    candidates = draw_candidates(jax.random.fold_in(jax.random.fold_in(key_list[7], part), 71), part)
    codes = plant(jax.random.randint(part_keys[2], (PASSAGES, PLEN), 0, CENT_DEV), jax.random.fold_in(part_keys[2], 1), 0, CENT_DEV - 1).astype(jnp.int32)
    residual_words = draw_residual_words(jax.random.fold_in(jax.random.fold_in(key_list[7], part), 71), part)
    lengths = draw_lengths(jax.random.fold_in(jax.random.fold_in(key_list[7], part), 71), part)
    centroids = centred(part_keys[5], (CENTROIDS, D), D ** -0.5, 0.5, ((0, 16),), jnp.float32)
    bucket_values = centred(key_list[6], (4, D), (0.7 / D ** 0.5), 0.35355338, (), jnp.float32)
    return {"queries": queries, "candidates": candidates, "codes": codes, "residual_words": residual_words, "lengths": lengths, "centroids": centroids, "bucket_values": bucket_values}


epsilon = 1e-06

def unit_rows(values_in):
    values = values_in.astype(jnp.float32)
    return values / jnp.sqrt(lax.optimization_barrier(jnp.sum(values * values, axis=-1, keepdims=True)) + epsilon)

def decode(codes, words, centroids, bucket_values):
    width = centroids.shape[1]
    expanded = jnp.repeat(words, 8, axis=-2)[..., :width, :]
    powers = jnp.power(4, jnp.arange(width, dtype=jnp.int32) % 8).astype(jnp.int32)
    buckets = jnp.swapaxes(expanded // powers[:, None] % 4, -1, -2)
    residual = jnp.zeros(buckets.shape, jnp.float32)
    for level in range(4):
        residual = residual + jnp.where(buckets == level, bucket_values[level], jnp.float32(0.0))
    vectors = centroids[codes] + residual
    return unit_rows(vectors).astype(jnp.bfloat16)

def maxsim(query_group, vectors, slot_lengths, slot_ids):
    similar = jnp.einsum('bid,bcjd->bcij', query_group.astype(jnp.float32), vectors.astype(jnp.float32), precision=lax.Precision.HIGHEST)
    positions = jnp.arange(vectors.shape[2], dtype=jnp.int32)
    within = positions[None, None, :] < slot_lengths[:, :, None]
    maxima = lax.optimization_barrier(jnp.max(jnp.where(within[:, :, None, :], similar, jnp.float32(-1e+30)), axis=-1))
    return jnp.where(slot_ids >= 0, lax.optimization_barrier(jnp.mean(maxima, axis=-1)), jnp.float32(0.0))

def reference(queries, candidates, codes, residual_words, lengths, centroids, bucket_values):
    query_unit = unit_rows(queries).astype(jnp.bfloat16)
    by_owner = (codes.reshape(N_WIDE, P_DEV, PLEN), residual_words.reshape(N_WIDE, P_DEV, RWORDS, PLEN), lengths.reshape(N_WIDE, P_DEV), centroids.reshape(N_WIDE, CENT_DEV, D), jnp.transpose(candidates.reshape(QUERIES, N_WIDE, CAND), (1, 0, 2)))

    def owner_scores(owned):
        own_codes, own_words, own_lengths, own_centroids, slot_ids = owned
        decoded = decode(own_codes, own_words, own_centroids, bucket_values)
        clipped = jnp.maximum(slot_ids, 0).astype(jnp.int32)
        return maxsim(query_unit, decoded[clipped], own_lengths[clipped], slot_ids)
    owner_table = lax.map(owner_scores, by_owner)
    return jnp.transpose(owner_table, (1, 0, 2)).reshape(QUERIES, N_WIDE * CAND)
```

```python
import functools

import jax
import jax.numpy as jnp
from jax import lax
from jax.experimental import pallas as pl
from jax.experimental.pallas import tpu as pltpu
from jax.sharding import PartitionSpec as P

epsilon = 1e-06
MESH = pl.DeviceIdType.MESH


def kernel(n, q_ref, cand_ref, codes_ref, words_ref, len_ref, cent_ref, bv_ref, out_ref,
           allq, flat, pick4, raw_a, raw_b, dec, best, snd, rcv,
           send1, recv1, send2, recv2, send3, recv3):
    chips = n // 2
    me = lax.axis_index("wide")
    chip, core = me // 2, lax.rem(me, 2)
    sibling = chip * 2 + 1 - core
    passages, plen = codes_ref.shape
    rows = q_ref.shape[0]
    width = q_ref.shape[1]
    cand = cand_ref.shape[1]
    per = snd.shape[1]

    barrier = pltpu.get_barrier_semaphore()

    def greet(step, carry):
        pl.semaphore_signal(barrier, inc=1, device_id={"wide": lax.rem(me + step, n)}, device_id_type=MESH)
        return carry

    lax.fori_loop(1, n, greet, 0)

    q = q_ref[...].astype(jnp.float32)
    q = q * lax.rsqrt(jnp.sum(q * q, axis=-1, keepdims=True) + epsilon)
    allq[chip, core] = q.astype(jnp.bfloat16)

    pl.semaphore_wait(barrier, n - 1)

    def to_chip(step):
        other = lax.rem(chip + step, chips)
        return pltpu.make_async_remote_copy(
            src_ref=allq.at[chip, core], dst_ref=allq.at[chip, core],
            send_sem=send1.at[other], recv_sem=recv1.at[chip],
            device_id={"wide": other * 2 + core}, device_id_type=MESH)

    def from_chip(step):
        other = lax.rem(chip + step, chips)
        return pltpu.make_async_remote_copy(
            src_ref=allq.at[other, core], dst_ref=allq.at[other, core],
            send_sem=send1.at[other], recv_sem=recv1.at[other],
            device_id={"wide": other * 2 + core}, device_id_type=MESH)

    def to_sibling(step):
        other = lax.rem(chip + step, chips)
        return pltpu.make_async_remote_copy(
            src_ref=allq.at[other, core], dst_ref=allq.at[other, core],
            send_sem=send2.at[other], recv_sem=recv2.at[other],
            device_id={"wide": sibling}, device_id_type=MESH)

    def from_sibling(step):
        other = lax.rem(chip + step, chips)
        return pltpu.make_async_remote_copy(
            src_ref=allq.at[other, 1 - core], dst_ref=allq.at[other, 1 - core],
            send_sem=send2.at[other], recv_sem=recv2.at[other],
            device_id={"wide": sibling}, device_id_type=MESH)

    for step in range(1, chips):
        to_chip(step).start()
    to_sibling(0).start()

    row = lax.broadcasted_iota(jnp.int32, (128, width), 0)
    col = lax.broadcasted_iota(jnp.int32, (128, width), 1)
    holds = (row % 16 == col // 8) & ((row // 16) % 2 == (col // 4) % 2)
    for inner in range(4):
        pick4[inner] = jnp.where(holds & (row // 32 == inner), 1.0, 0.0).astype(jnp.bfloat16)

    def turn(group, carry):
        parts = []
        for inner in range(4):
            word = words_ref[group * 4 + inner]
            parts += [word & 255, word >> 8]
        both = jnp.concatenate(parts, axis=0).astype(jnp.float32)
        flat[group] = jnp.transpose(both).astype(jnp.bfloat16)
        return carry

    lax.fori_loop(0, passages // 4, turn, 0)

    shift = 2 * (lax.broadcasted_iota(jnp.int32, (plen, width), 1) % 4)
    low_bit = jnp.left_shift(jnp.int32(1), shift)
    high_bit = jnp.left_shift(jnp.int32(2), shift)
    place = lax.broadcasted_iota(jnp.int32, (plen, width), 0)

    def fetch(p, raw):
        for start in range(0, plen, 8):
            got = [cent_ref[codes_ref[p, start + j]] for j in range(8)]
            for j in range(8):
                raw[start + j:start + j + 1, :] = got[j]

    def decode(p, raw):
        byte = jnp.dot(flat[p // 4], pick4[lax.rem(p, 4)], preferred_element_type=jnp.float32).astype(jnp.int32)
        low = (byte & low_bit) != 0
        high = (byte & high_bit) != 0
        residual = jnp.where(high, jnp.where(low, bv_ref[3:4, :], bv_ref[2:3, :]),
                             jnp.where(low, bv_ref[1:2, :], bv_ref[0:1, :]))
        value = raw[...] + residual
        value = jnp.where(place < len_ref[p], value, value[0:1, :])
        value = value * lax.rsqrt(jnp.sum(value * value, axis=-1, keepdims=True) + epsilon)
        dec[pl.ds(pl.multiple_of(p * plen, plen), plen), :] = value.astype(jnp.bfloat16)

    def pair(i, carry):
        fetch(2 * i + 1, raw_b)
        decode(2 * i, raw_a)
        fetch(jnp.minimum(2 * i + 2, passages - 1), raw_a)
        decode(2 * i + 1, raw_b)
        return carry

    fetch(0, raw_a)
    half = passages // 4
    lax.fori_loop(0, half, pair, 0)
    for step in range(1, chips):
        from_chip(step).wait_recv()
        to_sibling(step).start()
    lax.fori_loop(half, passages // 2, pair, 0)
    for step in range(chips):
        from_sibling(step).wait_recv()

    group = 8
    groups = passages // group

    def score(k, carry):
        tile = allq[k].reshape(2 * rows, width)
        for g in range(groups):
            similar = lax.dot_general(dec[g * group * plen:(g + 1) * group * plen, :], tile,
                                      (((1,), (1,)), ((), ())), preferred_element_type=jnp.float32)
            best[k, g * group:(g + 1) * group, :] = jnp.max(similar.reshape(group, plen, 2 * rows), axis=1)
        return carry

    lax.fori_loop(0, chips, score, 0)

    held = 2 * per
    tokens = rows // per
    qrow = lax.broadcasted_iota(jnp.int32, (held, 2 * rows), 0)
    qcol = lax.broadcasted_iota(jnp.int32, (held, 2 * rows), 1)
    mean = jnp.where(qcol // tokens == qrow, 1.0 / tokens, 0.0).astype(jnp.bfloat16)
    lanes = snd.shape[2]
    lane = lax.broadcasted_iota(jnp.int32, (held, lanes), 1)
    slot = lane - me * cand
    ids = lax.broadcasted_iota(jnp.int32, (held, passages), 1)

    def finish(k, carry):
        full = best[k]
        top = full.astype(jnp.bfloat16)
        rest = full - top.astype(jnp.float32)
        mid = rest.astype(jnp.bfloat16)
        low = (rest - mid.astype(jnp.float32)).astype(jnp.bfloat16)
        dims = (((1,), (1,)), ((), ()))
        scores = sum(lax.dot_general(mean, part, dims, preferred_element_type=jnp.float32)
                     for part in (low, mid, top))
        chosen = cand_ref[pl.ds(pl.multiple_of(k * held, held), held), :]
        block = jnp.zeros((held, lanes), jnp.float32)
        for s in range(cand):
            one = jnp.sum(jnp.where(chosen[:, s:s + 1] == ids, scores, 0.0), axis=1, keepdims=True)
            block = jnp.where(slot == s, one, block)
        snd[2 * k] = block[:per]
        snd[2 * k + 1] = block[per:]
        return carry

    lax.fori_loop(0, chips, finish, 0, unroll=True if chips <= 8 else 4)

    def to_owner(step):
        other = lax.rem(me + step, n)
        return pltpu.make_async_remote_copy(
            src_ref=snd.at[other], dst_ref=rcv.at[me],
            send_sem=send3.at[other], recv_sem=recv3.at[me],
            device_id={"wide": other}, device_id_type=MESH)

    def from_owner(step):
        other = lax.rem(me + step, n)
        return pltpu.make_async_remote_copy(
            src_ref=snd.at[other], dst_ref=rcv.at[other],
            send_sem=send3.at[other], recv_sem=recv3.at[other],
            device_id={"wide": other}, device_id_type=MESH)

    for step in range(1, n):
        to_owner(step).start()
    rcv[me] = snd[me]
    for step in range(1, n):
        from_owner(step).wait_recv()
    total = rcv[0]
    for o in range(1, n):
        total = total + rcv[o]
    out_ref[...] = total[:, :out_ref.shape[1]]

    for step in range(1, chips):
        to_chip(step).wait_send()
    for step in range(chips):
        to_sibling(step).wait_send()
    for step in range(1, n):
        to_owner(step).wait_send()


def on_device(n, queries, candidates, codes, residual_words, lengths, centroids, bucket_values):
    per, tokens, width = queries.shape
    passages, plen = codes.shape
    chips = n // 2
    slots = n * candidates.shape[1]
    lanes = -(-slots // 128) * 128
    rows = per * tokens
    vmem = pl.BlockSpec(memory_space=pltpu.VMEM)
    smem = pl.BlockSpec(memory_space=pltpu.SMEM)
    dma = pltpu.SemaphoreType.DMA
    return pl.pallas_call(
        functools.partial(kernel, n),
        out_shape=jax.ShapeDtypeStruct((per, slots), jnp.float32),
        in_specs=[vmem, vmem, smem, vmem, smem, vmem, vmem],
        out_specs=vmem,
        scratch_shapes=[
            pltpu.VMEM((chips, 2, rows, width), jnp.bfloat16),
            pltpu.VMEM((passages // 4, plen, 128), jnp.bfloat16),
            pltpu.VMEM((4, 128, width), jnp.bfloat16),
            pltpu.VMEM((plen, width), jnp.float32),
            pltpu.VMEM((plen, width), jnp.float32),
            pltpu.VMEM((passages * plen, width), jnp.bfloat16),
            pltpu.VMEM((chips, passages, 2 * rows), jnp.float32),
            pltpu.VMEM((n, per, lanes), jnp.float32),
            pltpu.VMEM((n, per, lanes), jnp.float32),
            dma((chips,)), dma((chips,)), dma((chips,)), dma((chips,)), dma((n,)), dma((n,)),
        ],
        compiler_params=pltpu.CompilerParams(
            collective_id=0, has_side_effects=True, vmem_limit_bytes=48 * 1024 * 1024),
    )(queries.reshape(rows, width), candidates, codes, residual_words, lengths,
      centroids.reshape(centroids.shape[0], 1, width), bucket_values)


def solution(mesh):
    in_specs = (
        P(("groups", "wide"), None, None),
        P("groups", "wide"),
        P(("groups", "wide"), None),
        P(("groups", "wide"), None, None),
        P(("groups", "wide")),
        P(("groups", "wide"), None),
        P(),
    )
    return jax.shard_map(
        functools.partial(on_device, mesh.shape["wide"]), mesh=mesh, in_specs=in_specs,
        out_specs=P(("groups", "wide"), None), check_vma=False
    )
```

```python
import functools

import jax
import jax.numpy as jnp
from jax import lax
from jax.experimental import pallas as pl
from jax.experimental.pallas import tpu as pltpu
from jax.sharding import PartitionSpec as P

epsilon = 1e-06
MESH = pl.DeviceIdType.MESH


def kernel(n, q_hbm, cand_hbm, codes_hbm, words_hbm, len_hbm, cent_hbm, bv_hbm, out_ref,
           q_ref, cand_ref, codes_ref, words_ref, len_ref, cent_ref, bv_ref, load_sem, chosen_ref, allq, flat, pick4, raw_a, raw_b, dec, best, snd, rcv,
           send1, recv1, send2, recv2, send3, recv3):
    chips = n // 2
    me = lax.axis_index("wide")
    chip, core = me // 2, lax.rem(me, 2)
    sibling = chip * 2 + 1 - core
    passages, plen = codes_ref.shape
    rows = q_ref.shape[0]
    width = q_ref.shape[1]
    cand = cand_ref.shape[0]
    per = snd.shape[1]

    pairs = ((q_hbm, q_ref), (cent_hbm, cent_ref), (words_hbm, words_ref), (codes_hbm, codes_ref),
             (len_hbm, len_ref), (bv_hbm, bv_ref), (cand_hbm, cand_ref))
    loads = [pltpu.make_async_copy(a, b, load_sem.at[i]) for i, (a, b) in enumerate(pairs)]
    for load in loads:
        load.start()

    barrier = pltpu.get_barrier_semaphore()

    def greet(step, carry):
        pl.semaphore_signal(barrier, inc=1, device_id={"wide": lax.rem(me + step, n)}, device_id_type=MESH)
        return carry

    lax.fori_loop(1, n, greet, 0)

    loads[0].wait()
    q = q_ref[...].astype(jnp.float32)
    q = q * lax.rsqrt(jnp.sum(q * q, axis=-1, keepdims=True) + epsilon)
    allq[chip, core] = q.astype(jnp.bfloat16)

    def to_chip(step):
        other = lax.rem(chip + step, chips)
        return pltpu.make_async_remote_copy(
            src_ref=allq.at[chip, core], dst_ref=allq.at[chip, core],
            send_sem=send1.at[other], recv_sem=recv1.at[chip],
            device_id={"wide": other * 2 + core}, device_id_type=MESH)

    def from_chip(step):
        other = lax.rem(chip + step, chips)
        return pltpu.make_async_remote_copy(
            src_ref=allq.at[other, core], dst_ref=allq.at[other, core],
            send_sem=send1.at[other], recv_sem=recv1.at[other],
            device_id={"wide": other * 2 + core}, device_id_type=MESH)

    def to_sibling(step):
        other = lax.rem(chip + step, chips)
        return pltpu.make_async_remote_copy(
            src_ref=allq.at[other, core], dst_ref=allq.at[other, core],
            send_sem=send2.at[other], recv_sem=recv2.at[other],
            device_id={"wide": sibling}, device_id_type=MESH)

    def from_sibling(step):
        other = lax.rem(chip + step, chips)
        return pltpu.make_async_remote_copy(
            src_ref=allq.at[other, 1 - core], dst_ref=allq.at[other, 1 - core],
            send_sem=send2.at[other], recv_sem=recv2.at[other],
            device_id={"wide": sibling}, device_id_type=MESH)

    for load in loads[1:]:
        load.wait()
    chosen_ref[...] = jnp.transpose(cand_ref[...])

    row = lax.broadcasted_iota(jnp.int32, (128, width), 0)
    col = lax.broadcasted_iota(jnp.int32, (128, width), 1)
    holds = (row % 16 == col // 8) & ((row // 16) % 2 == (col // 4) % 2)
    for inner in range(4):
        pick4[:, inner * width:(inner + 1) * width] = jnp.where(holds & (row // 32 == inner), 1.0, 0.0).astype(jnp.bfloat16)

    def turn(group, carry):
        parts = []
        for inner in range(4):
            word = words_ref[group * 4 + inner]
            parts += [word & 255, word >> 8]
        both = jnp.concatenate(parts, axis=0).astype(jnp.float32)
        flat[group] = jnp.transpose(both).astype(jnp.bfloat16)
        return carry

    lax.fori_loop(0, passages // 4, turn, 0)

    shift = 2 * (lax.broadcasted_iota(jnp.int32, (plen, width), 1) % 4)
    low_bit = jnp.left_shift(jnp.int32(1), shift)
    high_bit = jnp.left_shift(jnp.int32(2), shift)
    place = lax.broadcasted_iota(jnp.int32, (plen, width), 0)

    batch = 4

    def fetch(i, raw):
        for inner in range(batch):
            p = i * batch + inner
            for start in range(0, plen, 8):
                got = [cent_ref[codes_ref[p, start + j]] for j in range(8)]
                for j in range(8):
                    raw[inner * plen + start + j:inner * plen + start + j + 1, :] = got[j]

    def decode(i, raw):
        bytes4 = jnp.dot(flat[i], pick4[...], preferred_element_type=jnp.float32)
        for inner in range(batch):
            p = i * batch + inner
            byte = bytes4[:, inner * width:(inner + 1) * width].astype(jnp.int32)
            low = (byte & low_bit) != 0
            high = (byte & high_bit) != 0
            residual = jnp.where(high, jnp.where(low, bv_ref[3:4, :], bv_ref[2:3, :]),
                                 jnp.where(low, bv_ref[1:2, :], bv_ref[0:1, :]))
            value = raw[inner * plen:(inner + 1) * plen, :] + residual
            value = jnp.where(place < len_ref[p], value, value[0:1, :])
            value = value * lax.rsqrt(jnp.sum(value * value, axis=-1, keepdims=True) + epsilon)
            dec[pl.ds(pl.multiple_of(p * plen, plen), plen), :] = value.astype(jnp.bfloat16)

    last = passages // batch - 1

    def pair(i, carry):
        fetch(2 * i + 1, raw_b)
        decode(2 * i, raw_a)
        fetch(jnp.minimum(2 * i + 2, last), raw_a)
        decode(2 * i + 1, raw_b)
        return carry

    fetch(0, raw_a)
    early = 1
    lax.fori_loop(0, early, pair, 0)
    pl.semaphore_wait(barrier, n - 1)
    for step in range(1, chips):
        to_chip(step).start()
    to_sibling(0).start()
    lax.fori_loop(early, passages // (2 * batch), pair, 0)

    group = 8
    groups = passages // group

    def score(k):
        tile = allq[k].reshape(2 * rows, width)
        for g in range(groups):
            similar = lax.dot_general(dec[g * group * plen:(g + 1) * group * plen, :], tile,
                                      (((1,), (1,)), ((), ())), preferred_element_type=jnp.float32)
            best[k, g * group:(g + 1) * group, :] = jnp.max(similar.reshape(group, plen, 2 * rows), axis=1)

    held = 2 * per
    tokens = rows // per
    qrow = lax.broadcasted_iota(jnp.int32, (held, 2 * rows), 0)
    qcol = lax.broadcasted_iota(jnp.int32, (held, 2 * rows), 1)
    mean = jnp.where(qcol // tokens == qrow, 1.0 / tokens, 0.0).astype(jnp.bfloat16)
    lanes = snd.shape[2]
    lane = lax.broadcasted_iota(jnp.int32, (held, lanes), 1)
    slot = lane - me * cand
    ids = lax.broadcasted_iota(jnp.int32, (held, passages), 1)

    def finish(k):
        full = best[k]
        top = full.astype(jnp.bfloat16)
        rest = full - top.astype(jnp.float32)
        mid = rest.astype(jnp.bfloat16)
        low = (rest - mid.astype(jnp.float32)).astype(jnp.bfloat16)
        dims = (((1,), (1,)), ((), ()))
        scores = sum(lax.dot_general(mean, part, dims, preferred_element_type=jnp.float32)
                     for part in (low, mid, top))
        chosen = chosen_ref[pl.ds(pl.multiple_of(k * held, held), held), :]
        block = jnp.zeros((held, lanes), jnp.float32)
        for s in range(cand):
            one = jnp.sum(jnp.where(chosen[:, s:s + 1] == ids, scores, 0.0), axis=1, keepdims=True)
            block = jnp.where(slot == s, one, block)
        snd[2 * k] = block[:per]
        snd[2 * k + 1] = block[per:]

    def to_owner(other):
        return pltpu.make_async_remote_copy(
            src_ref=snd.at[other], dst_ref=rcv.at[me],
            send_sem=send3.at[other], recv_sem=recv3.at[me],
            device_id={"wide": other}, device_id_type=MESH)

    def from_owner(other):
        return pltpu.make_async_remote_copy(
            src_ref=snd.at[other], dst_ref=rcv.at[other],
            send_sem=send3.at[other], recv_sem=recv3.at[other],
            device_id={"wide": other}, device_id_type=MESH)

    def forward(step):
        from_chip(step).wait_recv()
        to_sibling(step).start()

    def chip_at(i):
        return lax.rem(chip + chips - i, chips)

    ahead = min(2, chips - 1)
    for i in range(1, ahead + 1):
        forward(chips - i)
    from_sibling(0).wait_recv()
    score(chip)

    def turn_out(i, carry):
        @pl.when(i + ahead < chips)
        def _():
            forward(chips - i - ahead)

        from_sibling(chips - i).wait_recv()
        score(chip_at(i))
        before = chip_at(i - 1)
        finish(before)

        @pl.when(i == 1)
        def _():
            to_owner(sibling).start()

        @pl.when(i > 1)
        def _():
            to_owner(2 * before).start()
            to_owner(2 * before + 1).start()

        return carry

    lax.fori_loop(1, chips, turn_out, 0)
    final = chip_at(chips - 1)
    finish(final)
    to_owner(2 * final).start()
    to_owner(2 * final + 1).start()
    rcv[me] = snd[me]
    for step in range(1, n):
        from_owner(lax.rem(me + step, n)).wait_recv()
    total = rcv[0]
    for o in range(1, n):
        total = total + rcv[o]
    out_ref[...] = total[:, :out_ref.shape[1]]

    for step in range(1, chips):
        to_chip(step).wait_send()
    for step in range(chips):
        to_sibling(step).wait_send()
    for step in range(1, n):
        to_owner(lax.rem(me + step, n)).wait_send()


def on_device(n, queries, candidates, codes, residual_words, lengths, centroids, bucket_values):
    per, tokens, width = queries.shape
    passages, plen = codes.shape
    chips = n // 2
    slots = n * candidates.shape[1]
    lanes = -(-slots // 128) * 128
    rows = per * tokens
    vmem = pl.BlockSpec(memory_space=pltpu.VMEM)
    dma = pltpu.SemaphoreType.DMA
    return pl.pallas_call(
        functools.partial(kernel, n),
        out_shape=jax.ShapeDtypeStruct((per, slots), jnp.float32),
        in_specs=[pl.BlockSpec(memory_space=pltpu.HBM)] * 7,
        out_specs=vmem,
        scratch_shapes=[
            pltpu.VMEM((rows, width), queries.dtype),
            pltpu.VMEM(candidates.shape[::-1], jnp.int32),
            pltpu.SMEM((passages, plen), jnp.int32),
            pltpu.VMEM(residual_words.shape, jnp.int32),
            pltpu.SMEM((passages,), jnp.int32),
            pltpu.VMEM((centroids.shape[0], 1, width), jnp.float32),
            pltpu.VMEM(bucket_values.shape, jnp.float32),
            dma((7,)),
            pltpu.VMEM(candidates.shape, jnp.int32),
            pltpu.VMEM((chips, 2, rows, width), jnp.bfloat16),
            pltpu.VMEM((passages // 4, plen, 128), jnp.bfloat16),
            pltpu.VMEM((128, 4 * width), jnp.bfloat16),
            pltpu.VMEM((4 * plen, width), jnp.float32),
            pltpu.VMEM((4 * plen, width), jnp.float32),
            pltpu.VMEM((passages * plen, width), jnp.bfloat16),
            pltpu.VMEM((chips, passages, 2 * rows), jnp.float32),
            pltpu.VMEM((n, per, lanes), jnp.float32),
            pltpu.VMEM((n, per, lanes), jnp.float32),
            dma((chips,)), dma((chips,)), dma((chips,)), dma((chips,)), dma((n,)), dma((n,)),
        ],
        compiler_params=pltpu.CompilerParams(
            collective_id=0, has_side_effects=True, vmem_limit_bytes=48 * 1024 * 1024),
    )(queries.reshape(rows, width), candidates.T, codes, residual_words, lengths,
      centroids.reshape(centroids.shape[0], 1, width), bucket_values)


def solution(mesh):
    in_specs = (
        P(("groups", "wide"), None, None),
        P("groups", "wide"),
        P(("groups", "wide"), None),
        P(("groups", "wide"), None, None),
        P(("groups", "wide")),
        P(("groups", "wide"), None),
        P(),
    )
    return jax.shard_map(
        functools.partial(on_device, mesh.shape["wide"]), mesh=mesh, in_specs=in_specs,
        out_specs=P(("groups", "wide"), None), check_vma=False
    )
```

```python
import functools

import jax
import jax.numpy as jnp
from jax import lax
from jax.experimental import pallas as pl
from jax.experimental.pallas import tpu as pltpu
from jax.sharding import PartitionSpec as P

epsilon = 1e-06
MESH = pl.DeviceIdType.MESH


def kernel(n, q_hbm, cand_hbm, codes_hbm, words_hbm, len_hbm, cent_hbm, bv_hbm, out_ref,
           q_ref, cand_ref, codes_ref, words_ref, len_ref, cent_ref, bv_ref, load_sem, chosen_ref, allq, flat, pick4, raw_a, raw_b, dec, best, snd, rcv,
           send1, recv1, send2, recv2, send3, recv3):
    chips = n // 2
    me = lax.axis_index("wide")
    chip, core = me // 2, lax.rem(me, 2)
    sibling = chip * 2 + 1 - core
    passages, plen = codes_ref.shape
    rows = q_ref.shape[0]
    width = q_ref.shape[1]
    cand = cand_ref.shape[0]
    per = snd.shape[1]

    pairs = ((q_hbm, q_ref), (cent_hbm, cent_ref), (words_hbm, words_ref), (codes_hbm, codes_ref),
             (len_hbm, len_ref), (bv_hbm, bv_ref), (cand_hbm, cand_ref))
    loads = [pltpu.make_async_copy(a, b, load_sem.at[i]) for i, (a, b) in enumerate(pairs)]
    for load in loads:
        load.start()

    barrier = pltpu.get_barrier_semaphore()

    def greet(step, carry):
        pl.semaphore_signal(barrier, inc=1, device_id={"wide": lax.rem(me + step, n)}, device_id_type=MESH)
        return carry

    lax.fori_loop(1, n, greet, 0)

    loads[0].wait()
    q = q_ref[...].astype(jnp.float32)
    q = q * lax.rsqrt(jnp.sum(q * q, axis=-1, keepdims=True) + epsilon)
    allq[chip, core] = q.astype(jnp.bfloat16)

    def to_chip(step):
        other = lax.rem(chip + step, chips)
        return pltpu.make_async_remote_copy(
            src_ref=allq.at[chip, core], dst_ref=allq.at[chip, core],
            send_sem=send1.at[other], recv_sem=recv1.at[chip],
            device_id={"wide": other * 2 + core}, device_id_type=MESH)

    def from_chip(step):
        other = lax.rem(chip + step, chips)
        return pltpu.make_async_remote_copy(
            src_ref=allq.at[other, core], dst_ref=allq.at[other, core],
            send_sem=send1.at[other], recv_sem=recv1.at[other],
            device_id={"wide": other * 2 + core}, device_id_type=MESH)

    def to_sibling(step):
        other = lax.rem(chip + step, chips)
        return pltpu.make_async_remote_copy(
            src_ref=allq.at[other, core], dst_ref=allq.at[other, core],
            send_sem=send2.at[other], recv_sem=recv2.at[other],
            device_id={"wide": sibling}, device_id_type=MESH)

    def from_sibling(step):
        other = lax.rem(chip + step, chips)
        return pltpu.make_async_remote_copy(
            src_ref=allq.at[other, 1 - core], dst_ref=allq.at[other, 1 - core],
            send_sem=send2.at[other], recv_sem=recv2.at[other],
            device_id={"wide": sibling}, device_id_type=MESH)

    for load in loads[1:]:
        load.wait()
    chosen_ref[...] = jnp.transpose(cand_ref[...])

    row = lax.broadcasted_iota(jnp.int32, (128, width), 0)
    col = lax.broadcasted_iota(jnp.int32, (128, width), 1)
    holds = (row % 16 == col // 8) & ((row // 16) % 2 == (col // 4) % 2)
    for inner in range(4):
        pick4[:, inner * width:(inner + 1) * width] = jnp.where(holds & (row // 32 == inner), 1.0, 0.0).astype(jnp.bfloat16)

    def turn(group, carry):
        parts = []
        for inner in range(4):
            word = words_ref[group * 4 + inner]
            parts += [word & 255, word >> 8]
        both = jnp.concatenate(parts, axis=0).astype(jnp.float32)
        flat[group] = jnp.transpose(both).astype(jnp.bfloat16)
        return carry

    lax.fori_loop(0, passages // 4, turn, 0)

    shift = 2 * (lax.broadcasted_iota(jnp.int32, (plen, width), 1) % 4)
    low_bit = jnp.left_shift(jnp.int32(1), shift)
    high_bit = jnp.left_shift(jnp.int32(2), shift)
    place = lax.broadcasted_iota(jnp.int32, (plen, width), 0)

    batch = 4

    def fetch(i, raw):
        for inner in range(batch):
            p = i * batch + inner
            for start in range(0, plen, 8):
                got = [cent_ref[codes_ref[p, start + j]] for j in range(8)]
                for j in range(8):
                    raw[inner * plen + start + j:inner * plen + start + j + 1, :] = got[j]

    def decode(i, raw):
        bytes4 = jnp.dot(flat[i], pick4[...], preferred_element_type=jnp.float32)
        for inner in range(batch):
            p = i * batch + inner
            byte = bytes4[:, inner * width:(inner + 1) * width].astype(jnp.int32)
            low = (byte & low_bit) != 0
            high = (byte & high_bit) != 0
            residual = jnp.where(high, jnp.where(low, bv_ref[3:4, :], bv_ref[2:3, :]),
                                 jnp.where(low, bv_ref[1:2, :], bv_ref[0:1, :]))
            value = raw[inner * plen:(inner + 1) * plen, :] + residual
            value = jnp.where(place < len_ref[p], value, value[0:1, :])
            value = value * lax.rsqrt(jnp.sum(value * value, axis=-1, keepdims=True) + epsilon)
            dec[pl.ds(pl.multiple_of(p * plen, plen), plen), :] = value.astype(jnp.bfloat16)

    last = passages // batch - 1

    def pair(i, carry):
        fetch(2 * i + 1, raw_b)
        decode(2 * i, raw_a)
        fetch(jnp.minimum(2 * i + 2, last), raw_a)
        decode(2 * i + 1, raw_b)
        return carry

    fetch(0, raw_a)
    early = 1
    lax.fori_loop(0, early, pair, 0)
    pl.semaphore_wait(barrier, n - 1)
    for step in range(1, chips):
        to_chip(step).start()
    to_sibling(0).start()
    lax.fori_loop(early, passages // (2 * batch), pair, 0)

    group = 8
    groups = passages // group

    def score(k):
        tile = allq[k].reshape(2 * rows, width)
        for g in range(groups):
            similar = lax.dot_general(dec[g * group * plen:(g + 1) * group * plen, :], tile,
                                      (((1,), (1,)), ((), ())), preferred_element_type=jnp.float32)
            best[k, g * group:(g + 1) * group, :] = jnp.max(similar.reshape(group, plen, 2 * rows), axis=1)

    held = 2 * per
    tokens = rows // per
    qrow = lax.broadcasted_iota(jnp.int32, (held, 2 * rows), 0)
    qcol = lax.broadcasted_iota(jnp.int32, (held, 2 * rows), 1)
    mean = jnp.where(qcol // tokens == qrow, 1.0 / tokens, 0.0).astype(jnp.bfloat16)
    lanes = snd.shape[2]
    lane = lax.broadcasted_iota(jnp.int32, (held, lanes), 1)
    slot = lane - me * cand
    ids = lax.broadcasted_iota(jnp.int32, (held, passages), 1)

    def finish(k):
        full = best[k]
        top = full.astype(jnp.bfloat16)
        rest = full - top.astype(jnp.float32)
        mid = rest.astype(jnp.bfloat16)
        low = (rest - mid.astype(jnp.float32)).astype(jnp.bfloat16)
        dims = (((1,), (1,)), ((), ()))
        scores = sum(lax.dot_general(mean, part, dims, preferred_element_type=jnp.float32)
                     for part in (low, mid, top))
        chosen = chosen_ref[pl.ds(pl.multiple_of(k * held, held), held), :]
        block = jnp.zeros((held, lanes), jnp.float32)
        for s in range(cand):
            one = jnp.sum(jnp.where(chosen[:, s:s + 1] == ids, scores, 0.0), axis=1, keepdims=True)
            block = jnp.where(slot == s, one, block)
        snd[2 * k] = block[:per]
        snd[2 * k + 1] = block[per:]

    def to_owner(other):
        return pltpu.make_async_remote_copy(
            src_ref=snd.at[other], dst_ref=rcv.at[me],
            send_sem=send3.at[other], recv_sem=recv3.at[me],
            device_id={"wide": other}, device_id_type=MESH)

    def from_owner(other):
        return pltpu.make_async_remote_copy(
            src_ref=snd.at[other], dst_ref=rcv.at[other],
            send_sem=send3.at[other], recv_sem=recv3.at[other],
            device_id={"wide": other}, device_id_type=MESH)

    def forward(step):
        from_chip(step).wait_recv()
        to_sibling(step).start()

    def chip_at(i):
        return lax.rem(chip + chips - i, chips)

    ahead = min(2, chips - 1)
    for i in range(1, min(ahead + 2, chips)):
        forward(chips - i)
    from_sibling(chips - 1).wait_recv()
    score(chip_at(1))

    def turn_out(i, carry):
        @pl.when(i + ahead < chips)
        def _():
            forward(chips - i - ahead)

        from_sibling(chips - i).wait_recv()
        score(chip_at(i))
        before = chip_at(i - 1)
        finish(before)

        to_owner(2 * before).start()
        to_owner(2 * before + 1).start()
        return carry

    lax.fori_loop(2, chips, turn_out, 0)
    from_sibling(0).wait_recv()
    score(chip)
    final = chip_at(chips - 1)
    finish(final)
    to_owner(2 * final).start()
    to_owner(2 * final + 1).start()
    finish(chip)
    to_owner(sibling).start()
    rcv[me] = snd[me]
    for step in range(1, n):
        from_owner(lax.rem(me + step, n)).wait_recv()
    total = rcv[0]
    for o in range(1, n):
        total = total + rcv[o]
    out_ref[...] = total[:, :out_ref.shape[1]]

    for step in range(1, chips):
        to_chip(step).wait_send()
    for step in range(chips):
        to_sibling(step).wait_send()
    for step in range(1, n):
        to_owner(lax.rem(me + step, n)).wait_send()


def on_device(n, queries, candidates, codes, residual_words, lengths, centroids, bucket_values):
    per, tokens, width = queries.shape
    passages, plen = codes.shape
    chips = n // 2
    slots = n * candidates.shape[1]
    lanes = -(-slots // 128) * 128
    rows = per * tokens
    vmem = pl.BlockSpec(memory_space=pltpu.VMEM)
    dma = pltpu.SemaphoreType.DMA
    return pl.pallas_call(
        functools.partial(kernel, n),
        out_shape=jax.ShapeDtypeStruct((per, slots), jnp.float32),
        in_specs=[pl.BlockSpec(memory_space=pltpu.HBM)] * 7,
        out_specs=vmem,
        scratch_shapes=[
            pltpu.VMEM((rows, width), queries.dtype),
            pltpu.VMEM(candidates.shape[::-1], jnp.int32),
            pltpu.SMEM((passages, plen), jnp.int32),
            pltpu.VMEM(residual_words.shape, jnp.int32),
            pltpu.SMEM((passages,), jnp.int32),
            pltpu.VMEM((centroids.shape[0], 1, width), jnp.float32),
            pltpu.VMEM(bucket_values.shape, jnp.float32),
            dma((7,)),
            pltpu.VMEM(candidates.shape, jnp.int32),
            pltpu.VMEM((chips, 2, rows, width), jnp.bfloat16),
            pltpu.VMEM((passages // 4, plen, 128), jnp.bfloat16),
            pltpu.VMEM((128, 4 * width), jnp.bfloat16),
            pltpu.VMEM((4 * plen, width), jnp.float32),
            pltpu.VMEM((4 * plen, width), jnp.float32),
            pltpu.VMEM((passages * plen, width), jnp.bfloat16),
            pltpu.VMEM((chips, passages, 2 * rows), jnp.float32),
            pltpu.VMEM((n, per, lanes), jnp.float32),
            pltpu.VMEM((n, per, lanes), jnp.float32),
            dma((chips,)), dma((chips,)), dma((chips,)), dma((chips,)), dma((n,)), dma((n,)),
        ],
        compiler_params=pltpu.CompilerParams(
            collective_id=0, has_side_effects=True, vmem_limit_bytes=48 * 1024 * 1024),
    )(queries.reshape(rows, width), candidates.T, codes, residual_words, lengths,
      centroids.reshape(centroids.shape[0], 1, width), bucket_values)


def solution(mesh):
    in_specs = (
        P(("groups", "wide"), None, None),
        P("groups", "wide"),
        P(("groups", "wide"), None),
        P(("groups", "wide"), None, None),
        P(("groups", "wide")),
        P(("groups", "wide"), None),
        P(),
    )
    return jax.shard_map(
        functools.partial(on_device, mesh.shape["wide"]), mesh=mesh, in_specs=in_specs,
        out_specs=P(("groups", "wide"), None), check_vma=False
    )
```
